32 devices in a mesh: row: 16 (over z, y, core), col: 2 (over x).
Axes of the slice: x: 2, y: 2, z: 4, core: 2. Of those that a mesh axis runs over, the one named last changes fastest.
Arguments:
- activations: bfloat16 [2, 512, 14848], P(None, 'row', 'col'), may hold values from -6 to 6
- output_gradient: bfloat16 [2, 512, 29696], P(None, 'col', 'row'), may hold values from -4 to 4
- weight: bfloat16 [14848, 29696], P('col', 'row'), may hold values from -0.046875 to 0.046875
Outputs:
- fisher: float32 [14848, 29696], P('col', 'row')
- activation_gradient: bfloat16 [2, 512, 14848], P(None, 'row', 'col')
The draws below stay inside these ranges and needn't reach their ends.
All inputs are finite; a program needn't handle non-finite values.
Results may differ from the reference program's by a relative error of at most 0.001.
Values may be sent and summed in bfloat16 or wider, within the bound.
A program may use at most 256 MiB of HBM per device.

```python
import jax
import jax.numpy as jnp
from jax import lax

D = 14848
FF = 29696
LENGTH = 512
SEQS = 2
N_ROW = 16


def spiked(result, stream_key, source, target, shards_of, factor):
    owner, partner = [(jnp.arange(result.shape[axis_at]) // (result.shape[axis_at] // shards_of)).reshape([-1 if axis == axis_at else 1 for axis in range(result.ndim)]) for axis_at in (source, target)]
    chosen = jax.random.permutation(stream_key, shards_of)[partner]
    strong = (owner == chosen) | (owner == (partner + shards_of // 2) % shards_of)
    return jnp.where(strong, factor * result, result)


def block_levels(stream_key, extent, cuts, low, high):
    def one(position, shards_of):
        draws = jax.random.uniform(jax.random.fold_in(jax.random.fold_in(stream_key, 6), position), (shards_of,), jnp.float32, low / len(cuts), high / len(cuts))
        return jnp.repeat(jnp.exp(draws), extent[position] // shards_of).reshape((-1,) + (1,) * (len(extent) - position - 1))

    gain = one(*cuts[0])
    for cut in cuts[1:]:
        gain = gain * one(*cut)
    return gain


def normal_values(own_key, dims, deviation, bound, cuts=(), kind=jnp.bfloat16):
    level = block_levels(own_key, dims, cuts, -0.22, 0.18) if cuts else 1.0
    entries = jax.random.normal(own_key, dims, jnp.float32) * deviation * level
    return jnp.minimum(jnp.maximum(entries, -bound), bound).astype(kind)


def heavy_noise(stream_key, extent, scale, most, cuts, heavy, kind=jnp.bfloat16):
    entries = scale * jax.random.normal(stream_key, extent, jnp.float32)
    if cuts:
        entries = entries * block_levels(stream_key, extent, cuts, -0.22, 0.18)
    return jnp.clip(spiked(entries, jax.random.fold_in(stream_key, 3), *heavy), -most, most).astype(kind)


def setup_inputs(seed: int = 0) -> dict:
    keys = jax.random.split(jax.random.key(seed), 4)
    return {
        "activations": normal_values(keys[0], (SEQS, LENGTH, D), 1.0, 6.0, ((1, 16), (2, 2))),
        "output_gradient": heavy_noise(keys[1], (SEQS, LENGTH, FF), 0.5, 4.0, ((1, 2), (2, 16)), (2, 1, 16, 2.0)),
        "weight": normal_values(keys[2], (D, FF), D ** -0.5, 0.046875, ((0, 2), (1, 16))),
    }


def reference(activations, output_gradient, weight):
    width = FF // N_ROW
    input_rows = activations.astype(jnp.float32)

    def column_block(index):
        column_slices = lax.dynamic_slice_in_dim(output_gradient, index * width, width, 2).astype(jnp.float32)
        gradient_list = jnp.einsum("qkc,qkh->qch", input_rows, column_slices, precision=lax.Precision.HIGHEST)
        return jnp.sum(gradient_list * gradient_list, axis=0) / (SEQS * LENGTH)

    blocks = lax.map(column_block, jnp.arange(N_ROW, dtype=jnp.int32))
    fisher = jnp.moveaxis(blocks, 0, 1).reshape(D, FF)
    activation_gradient = jnp.einsum("gkw,xw->gkx", output_gradient.astype(jnp.float32), weight.astype(jnp.float32), precision=lax.Precision.HIGHEST)
    return fisher, activation_gradient.astype(jnp.bfloat16)
```

```python
import jax
import jax.numpy as jnp
from jax import lax
from jax.experimental import pallas as pl
from jax.experimental.pallas import tpu as pltpu
from jax.sharding import PartitionSpec as P

SHARES = (6, 12, 17, 22, 26, 29)


def fisher_kernel(scale, g_ref, a_ref, o_ref):
    hidden = g_ref.shape[1]
    steps = next(n for n in (4, 2, 1) if hidden % (16 * n) == 0)
    rows = hidden // steps
    for i in range(steps):
        at = pl.ds(i * rows, rows)
        total = None
        for s in range(g_ref.shape[0]):
            grad = jnp.dot(g_ref[s, at, :], a_ref[s], preferred_element_type=jnp.float32)
            total = grad * grad if total is None else total + grad * grad
        o_ref[at, :] = total * scale


def fisher_of(g_t, act):
    seqs, hidden, length = g_t.shape
    width = act.shape[2]
    tile = 256 if width % 256 == 0 else width
    return pl.pallas_call(
        lambda *refs: fisher_kernel(1.0 / (seqs * length), *refs),
        grid=(width // tile,),
        in_specs=[
            pl.BlockSpec((seqs, hidden, length), lambda i: (0, 0, 0)),
            pl.BlockSpec((seqs, length, tile), lambda i: (0, 0, i)),
        ],
        out_specs=pl.BlockSpec((hidden, tile), lambda i: (0, i)),
        out_shape=jax.ShapeDtypeStruct((hidden, width), jnp.float32),
        cost_estimate=pl.CostEstimate(
            flops=2 * seqs * hidden * length * width,
            bytes_accessed=4 * hidden * width + 2 * seqs * length * (hidden + width),
            transcendentals=0,
        ),
        compiler_params=pltpu.CompilerParams(vmem_limit_bytes=48 * 2**20),
    )(g_t, act)


def cuts(width):
    unit = 256 if width % 256 == 0 else width
    count = width // unit
    edges = [0] + [unit * (count * n // SHARES[-1]) for n in SHARES]
    return [(low, high) for low, high in zip(edges[:-1], edges[1:]) if high > low], unit


def reduce_kernel(line, groups, pieces, unit, rows_ref, w_hbm, *refs):
    if groups == 2:
        g_hbm, out_ref, g_other_hbm, *scratch = refs
    else:
        out_ref, *scratch = refs
    count = len(pieces)
    held = scratch[:count]
    from_y = scratch[count : 2 * count]
    from_z = scratch[2 * count : 3 * count]
    w_buf, sums, rows_other = scratch[3 * count : 3 * count + 3]
    (w_sem, x_send, x_recv, c_send, c_recv, y_send, y_recv, z_send, z_recv) = scratch[3 * count + 3 :]
    half = rows_ref.shape[0] // 2
    quarter = half // 2
    span = line // groups
    chunk = quarter // span
    me = lax.axis_index("row")
    x = lax.axis_index("col")
    z, y, c = me // 4, lax.rem(me // 2, 2), lax.rem(me, 2)

    def row(z, y, c):
        return {"row": z * 4 + y * 2 + c}

    core_peer, y_peer = row(z, y, 1 - c), row(z, 1 - y, c)
    lower, upper = row(z - 1, y, c), row(z + 1, y, c)
    barrier = pltpu.get_barrier_semaphore()

    def greet(peer):
        pl.semaphore_signal(barrier, inc=1, device_id=peer, device_id_type=pl.DeviceIdType.MESH)

    greet(core_peer)
    greet(y_peer)
    if groups == 2:
        greet({"col": 1 - x})

    @pl.when(z > 0)
    def _():
        greet(lower)

    @pl.when(z < line - 1)
    def _():
        greet(upper)

    def load(k):
        low, high = pieces[k]
        return pltpu.make_async_copy(
            w_hbm.at[:, pl.ds(low, high - low)],
            w_buf.at[k % 2, :, pl.ds(0, high - low)],
            w_sem.at[k % 2],
        )

    for k in range(min(2, count)):
        load(k).start()
    pl.semaphore_wait(
        barrier, 1 + groups + jnp.where(z > 0, 1, 0) + jnp.where(z < line - 1, 1, 0)
    )

    def remote(src, dst, send, recv, peer):
        return pltpu.make_async_remote_copy(
            src_ref=src, dst_ref=dst, send_sem=send, recv_sem=recv,
            device_id=peer, device_id_type=pl.DeviceIdType.MESH,
        )

    if groups == 2:
        across = remote(rows_ref, rows_other, x_send.at[0], x_recv.at[0], {"col": 1 - x})
        across.start()
        across_whole = remote(
            g_hbm, g_other_hbm, x_send.at[1], x_recv.at[1], {"col": 1 - x}
        )

    if groups == 2 and count > 1:
        items = [(0, 0), (1, 0), (0, 1), (1, 1)]
        items += [(k, h) for k in range(2, count) for h in range(2)]
    else:
        items = [(k, h) for k in range(count) for h in range(groups)]

    def core_copy(i):
        k, h = items[i]
        width = pieces[k][1] - pieces[k][0]
        return remote(
            sums.at[i % 2, :, pl.ds(0, width)], held[k].at[h],
            c_send.at[i], c_recv.at[i], core_peer,
        )

    def y_copy(k, h):
        i = k * groups + h
        return remote(
            held[k].at[h, pl.ds(quarter, quarter), :], from_y[k].at[h],
            y_send.at[i], y_recv.at[i], y_peer,
        )

    def tiles(k, body):
        @pl.loop(0, (pieces[k][1] - pieces[k][0]) // unit)
        def _(i):
            body(pl.ds(pl.multiple_of(i * unit, unit), unit) if unit % 128 == 0 else slice(None))

    seen_w, seen_rows = set(), set([0])

    def send_sum(i):
        k, h = items[i]
        if k not in seen_w:
            seen_w.add(k)
            load(k).wait()
        if h not in seen_rows:
            seen_rows.add(h)
            across.wait_recv()
            across_whole.start()
        if i >= 2:
            core_copy(i - 2).wait_send()
        rows = rows_other if h else rows_ref

        def body(at):
            sums[i % 2, :, at] = jnp.dot(
                rows[pl.ds(half, half), :], w_buf[k % 2, :, at], preferred_element_type=jnp.float32
            )

        tiles(k, body)
        core_copy(i).start()

    def keep_sum(i):
        k, h = items[i]
        core_copy(i).wait_recv()
        rows = rows_other if h else rows_ref

        def body(at):
            held[k][h, :, at] += jnp.dot(
                rows[pl.ds(0, half), :], w_buf[k % 2, :, at], preferred_element_type=jnp.float32
            )

        tiles(k, body)
        y_copy(k, h).start()
        if h == groups - 1 and k + 2 < count:
            load(k + 2).start()

    def place(target):
        if groups == 2:
            return lax.rem(target // span + x, 2), lax.rem(target, span)
        return 0, target

    def z_copy(k, target, slot, peer):
        h, at = place(target)
        return remote(
            held[k].at[h, pl.ds(pl.multiple_of(at * chunk, chunk), chunk), :], from_z[k].at[slot],
            z_send.at[k, target], z_recv.at[k, slot], peer,
        )

    def add_arrived(k, target, slot):
        h, at = place(target)
        rows = pl.ds(pl.multiple_of(at * chunk, chunk), chunk)
        z_copy(k, target, slot, lower).wait_recv()
        held[k][h, rows, :] += from_z[k][slot]

    def rises(z, u):
        return z + u <= line - 1

    def take_y(k):
        for h in range(groups):
            y_copy(k, h).wait_recv()
            held[k][h, pl.ds(0, quarter), :] += from_y[k][h]

    def hop(k, u):
        @pl.when(rises(z, u))
        def _():
            @pl.when(z > 0)
            def _():
                add_arrived(k, z + u, z + u)

            z_copy(k, z + u, z + u, upper).start()

        @pl.when(z - u >= 0)
        def _():
            @pl.when(z < line - 1)
            def _():
                add_arrived(k, z - u, z - u)

            z_copy(k, z - u, line if u == 1 else z - u, lower).start()

    def finish(k):
        low, high = pieces[k]

        @pl.when(z > 0)
        def _():
            add_arrived(k, z, z)

        @pl.when(z < line - 1)
        def _():
            add_arrived(k, z, line)

        h, at = place(z)
        rows = pl.ds(pl.multiple_of(at * chunk, chunk), chunk)
        out_ref[:, low:high] = held[k][h, rows, :].astype(out_ref.dtype)

    def z_stage(n):
        for k in range(max(0, n - line), min(n, count - 1) + 1):
            if k == n:
                take_y(k)
            if n - k == line - 1:
                finish(k)
            elif n - k < line - 1:
                hop(k, line - 1 - (n - k))

    ahead = 0
    for i in range(len(items)):
        while ahead < len(items) and ahead <= i + 1:
            first_use = items[ahead][1] not in seen_rows or items[ahead][0] not in seen_w
            if ahead == i + 1 and first_use:
                break
            send_sum(ahead)
            ahead += 1
        keep_sum(i)
        k, h = items[i]
        if h == groups - 1 and k >= 2:
            z_stage(k - 2)
    for n in range(max(0, count - 2), count + line - 1):
        z_stage(n)

    if groups == 2:
        across.wait_send()
        across_whole.wait()
    for i in range(max(0, len(items) - 2), len(items)):
        core_copy(i).wait_send()
    for k in range(count):
        for h in range(groups):
            y_copy(k, h).wait_send()
        for target in range(line):

            @pl.when(z != target)
            def _():
                z_copy(k, target, target, lower).wait_send()


def reduce_of(rows, w_t, g_own, line, groups, seqs, block):
    hidden, width = w_t.shape
    pieces, unit = cuts(width)
    count = len(pieces)
    half = rows.shape[0] // 2
    widest = max(high - low for low, high in pieces)
    widths = [high - low for low, high in pieces]
    chunk = seqs * block
    dma = pltpu.SemaphoreType.DMA
    anywhere = pl.BlockSpec(memory_space=pl.ANY)
    whole = [g_own] if groups == 2 else []
    scratch = [pltpu.VMEM((groups, half, n), jnp.float32) for n in widths]
    scratch += [pltpu.VMEM((groups, half // 2, n), jnp.float32) for n in widths]
    scratch += [pltpu.VMEM((line + 1, chunk, n), jnp.float32) for n in widths]
    scratch += [
        pltpu.VMEM((2, hidden, widest), jnp.bfloat16),
        pltpu.VMEM((2, half, widest), jnp.float32),
        pltpu.VMEM((2 * half if groups == 2 else 16, hidden), jnp.bfloat16),
        dma((2,)), dma((2,)), dma((2,)),
        dma((groups * count,)), dma((groups * count,)),
        dma((groups * count,)), dma((groups * count,)),
        dma((count, line)), dma((count, line + 1)),
    ]
    return pl.pallas_call(
        lambda *refs: reduce_kernel(line, groups, pieces, unit, *refs),
        out_shape=[jax.ShapeDtypeStruct((chunk, width), jnp.bfloat16)]
        + [jax.ShapeDtypeStruct(g.shape, g.dtype) for g in whole],
        in_specs=[pl.BlockSpec(memory_space=pltpu.VMEM), anywhere] + [anywhere for _ in whole],
        out_specs=[pl.BlockSpec(memory_space=pltpu.VMEM)] + [anywhere for _ in whole],
        scratch_shapes=scratch,
        cost_estimate=pl.CostEstimate(
            flops=4 * groups * half * hidden * width * 2,
            bytes_accessed=2 * hidden * width,
            transcendentals=0,
        ),
        compiler_params=pltpu.CompilerParams(
            collective_id=0, has_side_effects=True, vmem_limit_bytes=60 * 2**20
        ),
    )(rows, w_t, *whole)


def make_local(n_row, n_col):
    line = n_row // 4

    def local(activations, output_gradient, weight):
        seqs, own, hidden = output_gradient.shape
        width = weight.shape[0]
        me = lax.axis_index("row")
        y, c = (me // 2) % 2, me % 2
        act = lax.all_gather(activations, "row", axis=1, tiled=True)
        g_own = jnp.swapaxes(output_gradient, 1, 2)
        groups = 2 if n_col == 2 and line % 2 == 0 else 1
        if groups == 2:
            group = output_gradient
        else:
            g_t = lax.all_gather(g_own, "col", axis=2, tiled=True)
            group = jnp.swapaxes(g_t, 1, 2)
        block = own * n_col // n_row

        span = line // groups
        g = group.reshape(seqs, span, 2, 2, block, hidden).transpose(3, 2, 1, 0, 4, 5)
        g = jnp.where(c == 0, g, g[::-1])
        g = jnp.where(y == 0, g, g[:, ::-1])
        rows = g.reshape(4 * span * seqs * block, hidden)
        grad, *others = reduce_of(rows, weight.T, g_own, line, groups, seqs, block)
        if groups == 2:
            first = lax.axis_index("col") == 0
            g_t = jnp.concatenate(
                [jnp.where(first, g_own, others[0]), jnp.where(first, others[0], g_own)], axis=2
            )
        return fisher_of(g_t, act).T, grad.reshape(seqs, block, width)

    return local


def solution(mesh):
    return jax.shard_map(
        make_local(mesh.shape["row"], mesh.shape["col"]),
        mesh=mesh,
        in_specs=(P(None, "row", "col"), P(None, "col", "row"), P("col", "row")),
        out_specs=(P("col", "row"), P(None, "row", "col")),
        check_vma=False,
    )
```
